32 devices in a mesh: band: 8 (over z, x), lev: 4 (over y, core).
Axes of the slice: x: 2, y: 2, z: 4, core: 2. Of those that a mesh axis runs over, the one named last changes fastest.
Arguments:
- columns: bfloat16 [65536, 274], P(('band', 'lev')), may hold values from -6 to 6
- departures: bfloat16 [4, 256, 128, 616], P('lev', 'band'), may hold values from -6 to 6
- jacobian: bfloat16 [274, 616], replicated, may hold values from -0.375 to 0.375
- chan_precision: bfloat16 [616, 616], replicated, as said below
- send_rows: int32 [32, 32, 4], P(('band', 'lev')), may hold values from 0 to 2047
- obs_slot: int32 [4, 256, 128], P('lev', 'band'), may hold values from 0 to 127
- counts: int32 [4, 256], P('lev', 'band'), may hold values from 16 to 128, as said below
Outputs:
- column_gradient: float32 [65536, 274], P(('band', 'lev'))
The draws below stay inside these ranges and needn't reach their ends.
Inputs may be any that keep to these rules, and one draw needn't show every extreme that they name: `send_rows`: each entry names a column of the sending device. `obs_slot`: each entry names one of the 128 slots, ordered by sending device then place. `counts`: each entry is 128 divided by 1, 2, 4 or 8; some entry equals 128. `chan_precision`: symmetric positive definite.
All inputs are finite; a program needn't handle non-finite values.
Results may differ from the reference program's by a relative error of at most 0.0018.
Values may be sent and summed in bfloat16 or wider, within the bound.
A program may use at most 128 MiB of HBM per device.

```python
import math
import jax
import jax.numpy as jnp
from jax import lax

CHAN = 616
PROF = 274
POS = 128
COLS_DEV = 2048
CAP = 4
LINES_DEV = 32
COLUMNS = 65536
SLOTS = 128
LINES = 256
N_LEV = 4
DEVICES = 32


def draw_chan_precision(key, part):
    first_key, second_key = jax.random.split(jax.random.fold_in(key, 17))
    diagonal = jnp.exp(jax.random.uniform(first_key, (CHAN,), jnp.float32, math.log(0.5), math.log(2.0)))
    noise = jax.random.normal(second_key, (CHAN, CHAN), jnp.float32) * (0.35 / (2.0 * math.sqrt(CHAN)))
    symmetric = noise + noise.T
    return (jnp.diag(diagonal) + symmetric).astype(jnp.bfloat16)


def draw_counts(key, part):
    shifts = jax.random.randint(jax.random.fold_in(key, 29), (N_LEV, LINES), 0, 4)
    values = POS // jnp.left_shift(jnp.ones((N_LEV, LINES), jnp.int32), shifts)
    return values.at[0, 0].set(POS).astype(jnp.int32)


def with_ends(array, rng, low, high):
    longest = array.shape.index(max(array.shape))
    spots = []
    for shift in (0, 1):
        where = [jax.random.randint(jax.random.fold_in(rng, axis), (), 0, length) for axis, length in enumerate(array.shape)]
        where[longest] = (where[longest] + shift) % array.shape[longest]
        spots.append(tuple(where))
    return array.at[spots[0]].set(low).at[spots[1]].set(high)


def level_of(stream_key, shape, cuts, least, largest):
    loudness, own = 1.0, jax.random.fold_in(stream_key, 6)
    for dim, shards_of in cuts:
        draws = jnp.exp(jax.random.uniform(jax.random.fold_in(own, dim), (shards_of,), jnp.float32, least / len(cuts), largest / len(cuts)))
        loudness = loudness * jnp.repeat(draws, shape[dim] // shards_of).reshape([-1 if axis == dim else 1 for axis in range(len(shape))])
    return loudness


def scatter_about(own_key, shape, spread, bound, shards=(), kind=jnp.bfloat16):
    result = spread * jax.random.normal(own_key, shape, jnp.float32)
    if shards:
        result = result * level_of(own_key, shape, shards, -0.22, 0.18)
    return jnp.clip(result, -bound, bound).astype(kind)


def setup_inputs(seed: int = 0) -> dict:
    keys = jax.random.split(jax.random.key(seed), 8)
    columns = scatter_about(keys[0], (COLUMNS, PROF), 1.0, 6.0, ((0, 32),))
    departures = scatter_about(keys[1], (N_LEV, LINES, POS, CHAN), 1.0, 6.0, ((0, 4), (1, 8)))
    jacobian = scatter_about(keys[2], (PROF, CHAN), PROF ** -0.5, 0.375)
    chan_precision = draw_chan_precision(jax.random.fold_in(keys[7], 71), 0)
    send_rows = with_ends(jax.random.randint(keys[4], (DEVICES, DEVICES, CAP), 0, COLS_DEV), jax.random.fold_in(keys[4], 1), 0, COLS_DEV - 1).astype(jnp.int32)
    obs_slot = with_ends(jax.random.randint(keys[5], (N_LEV, LINES, POS), 0, SLOTS), jax.random.fold_in(keys[5], 1), 0, SLOTS - 1).astype(jnp.int32)
    counts = draw_counts(jax.random.fold_in(keys[7], 71), 0)
    return {"columns": columns, "departures": departures, "jacobian": jacobian, "chan_precision": chan_precision, "send_rows": send_rows, "obs_slot": obs_slot, "counts": counts}


corr_length = 2.0


def reference(columns, departures, jacobian, chan_precision, send_rows, obs_slot, counts):
    decay_rate = math.exp(-1.0 / corr_length)
    norm_factor = 1.0 / (1.0 - decay_rate * decay_rate)
    positions = jnp.arange(POS, dtype=jnp.int32)

    def make_line(stream, line_index, line_slots, line_deps, line_count):
        observer = (line_index // LINES_DEV) * N_LEV + stream
        source = (line_slots // CAP).astype(jnp.int32)
        place = (line_slots % CAP).astype(jnp.int32)
        global_col = (source * COLS_DEV + send_rows[source, observer, place]).astype(jnp.int32)
        obs_columns = columns[global_col]
        model_equiv = jnp.dot(obs_columns, jacobian, preferred_element_type=jnp.float32)
        valid = positions < line_count
        residual = jnp.where(valid[:, None], model_equiv - line_deps.astype(jnp.float32), 0.0).astype(jnp.bfloat16)
        weighted = jnp.dot(residual, chan_precision, preferred_element_type=jnp.float32)
        return weighted, global_col, valid

    def finish_line(gradient, w_prev, w_cur, w_next, global_col, valid, line_index):
        at_end = (line_index == 0) | (line_index == LINES - 1)
        diag_value = jnp.where(at_end, norm_factor, (1.0 + decay_rate * decay_rate) * norm_factor)
        scaled = diag_value * w_cur - decay_rate * norm_factor * (w_prev + w_next)
        scaled = jnp.where(valid[:, None], scaled, 0.0).astype(jnp.bfloat16)
        obs_adjoint = lax.dot_general(scaled, jacobian, (((1,), (1,)), ((), ())), preferred_element_type=jnp.float32)
        return gradient.at[global_col].add(obs_adjoint)

    gradient = jnp.zeros((COLUMNS, PROF), jnp.float32)
    line_ids = jnp.arange(LINES, dtype=jnp.int32)
    for stream in range(N_LEV):
        def line_step(carry, inputs):
            gradient, w_prev, w_cur, col_cur, valid_cur, index_cur = carry
            line_slots, line_deps, line_count, line_index = inputs
            w_next, col_next, valid_next = make_line(stream, line_index, line_slots, line_deps, line_count)
            gradient = finish_line(gradient, w_prev, w_cur, w_next, col_cur, valid_cur, index_cur)
            return (gradient, w_cur, w_next, col_next, valid_next, line_index), None

        zero_line = jnp.zeros((POS, CHAN), jnp.float32)
        start = (gradient, zero_line, zero_line, jnp.zeros((POS,), jnp.int32), jnp.zeros((POS,), bool), jnp.int32(-1))
        carry, _ = lax.scan(line_step, start, (obs_slot[stream], departures[stream], counts[stream], line_ids))
        gradient, w_prev, w_cur, col_cur, valid_cur, index_cur = carry
        gradient = finish_line(gradient, w_prev, w_cur, zero_line, col_cur, valid_cur, index_cur)
    return gradient
```

```python
import functools
import math

import jax
import jax.numpy as jnp
from jax import lax
from jax.experimental import pallas as pl
from jax.experimental.pallas import tpu as pltpu
from jax.sharding import PartitionSpec as P

MESH = pl.DeviceIdType.MESH
corr_length = 2.0
F32, BF16 = jnp.float32, jnp.bfloat16


def halves(value):
    high = value.astype(BF16)
    return high, (value - high.astype(F32)).astype(BF16)


def across(left, right):
    return lax.dot_general(left, right, (((1,), (1,)), ((), ())), preferred_element_type=F32)


def plain(left, right):
    return jnp.dot(left, right, preferred_element_type=F32)


def hot(row, count):
    return jnp.where(lax.broadcasted_iota(jnp.int32, (count, row.shape[1]), 0) == row, 1.0, 0.0)


def picks(rows_ref, n_cols):
    n, cap = rows_ref.shape
    lanes = lax.broadcasted_iota(jnp.int32, (n, n_cols), 1)
    return jnp.concatenate(
        [jnp.where(lanes == rows_ref[:, c : c + 1], 1.0, 0.0) for c in range(cap)], axis=0
    ).astype(BF16)


def exchange(
    n_band, n_lev, group, cols, dep, jac, prec, rows, slots, counts, back,
    lines, padded, edge, edge_in, dep_in, wide, sent, got, gotf, mine, mine_in,
    obs, pair, small, total, dep_sem, entry_out, entry_in, col_out, col_in, row_out, row_in, adj_out, adj_in,
):
    decay = math.exp(-1.0 / corr_length)
    norm = 1.0 / (1.0 - decay * decay)
    inner, side = (1.0 + decay * decay) * norm, decay * norm
    n = n_band * n_lev
    n_lines, n_chan, n_pos = dep.shape
    cap, prof = sent.shape[1], sent.shape[2]
    n_slots = n * cap
    band, lev = lax.axis_index("band"), lax.axis_index("lev")
    me = band * n_lev + lev
    has_prev, has_next = band > 0, band < n_band - 1

    barrier = pltpu.get_barrier_semaphore()

    def greet(step, carry):
        other = lax.rem(me + step, n)
        pl.semaphore_signal(
            barrier, inc=1, device_id=(other // n_lev, lax.rem(other, n_lev)), device_id_type=MESH
        )
        return carry

    lax.fori_loop(1, n, greet, 0)

    n_groups = n_lines // group

    def load(g):
        part = pl.ds(g * group, group)
        return pltpu.make_async_copy(dep.at[part], lines.at[part], dep_sem.at[g])

    for g in range(n_groups):
        load(g).start()

    gathered = across(picks(rows, cols.shape[1]), cols[...])
    for c in range(cap):
        wide[:, c, :] = gathered[c * n : (c + 1) * n]
    sent[...] = wide[...].astype(BF16)
    got[me] = sent[me]

    numbers = slots[...]
    ordered = lax.rem(numbers, cap) * n + lax.div(numbers, cap)
    place = lax.broadcasted_iota(jnp.int32, (n_lines, n_pos), 1)
    ordered = jnp.where(place < counts[...], ordered, -1)
    nothing = jnp.full((8, n_pos), -1, jnp.int32)
    padded[0:8] = nothing
    padded[8 : 8 + n_lines] = ordered
    padded[8 + n_lines : 16 + n_lines] = nothing
    edge[0] = jnp.broadcast_to(ordered[0:1], (8, n_pos))
    edge[1] = jnp.broadcast_to(ordered[n_lines - 1 : n_lines], (8, n_pos))

    pl.semaphore_wait(barrier, n - 1)

    def scatter(blocks, target, out_sem, in_sem):
        def send(step, carry):
            other = lax.rem(me + step, n)
            pltpu.make_async_remote_copy(
                src_ref=blocks.at[other], dst_ref=target.at[me], send_sem=out_sem, recv_sem=in_sem,
                device_id=(other // n_lev, lax.rem(other, n_lev)), device_id_type=MESH,
            ).start()
            return carry

        lax.fori_loop(1, n, send, 0)

    def settle(blocks, sem):
        others = blocks.at[pl.ds(0, n - 1)]
        pltpu.make_async_copy(others, others, sem).wait()

    scatter(sent, got, col_out, col_in)

    def entries(to):
        line = 0 if to == 0 else n_lines - 1
        other = (band - 1 if to == 0 else band + 1, lev)
        place = 1 - to
        return (
            pltpu.make_async_remote_copy(
                src_ref=dep.at[line], dst_ref=dep_in.at[place], send_sem=entry_out.at[to],
                recv_sem=entry_in.at[place], device_id=other, device_id_type=MESH),
            pltpu.make_async_remote_copy(
                src_ref=edge.at[to], dst_ref=edge_in.at[place], send_sem=entry_out.at[2 + to],
                recv_sem=entry_in.at[2 + place], device_id=other, device_id_type=MESH),
        )

    def columns_to(to):
        other = (band - 1 if to == 0 else band + 1, lev)
        return pltpu.make_async_remote_copy(
            src_ref=mine, dst_ref=mine_in.at[1 - to], send_sem=row_out.at[to],
            recv_sem=row_in.at[1 - to], device_id=other, device_id_type=MESH)

    neighbours = ((0, has_prev), (1, has_next))
    for to, there in neighbours:
        @pl.when(there)
        def _(to=to):
            for copy in entries(to):
                copy.start()

    obs[...] = jnp.zeros_like(obs)
    pair[...] = jnp.zeros_like(pair)

    def add_group(g, carry):
        load(g).wait()
        near = padded[pl.ds(pl.multiple_of(g * group, 8), group + 16)]
        own, both, data = [], [], []
        for j in range(group):
            here = near[8 + j : 9 + j]
            before = jnp.where(here >= 0, near[7 + j : 8 + j], -1)
            after = jnp.where(here >= 0, near[9 + j : 10 + j], -1)
            own.append(hot(here, n_slots).astype(BF16))
            both.append((hot(before, n_slots) + hot(after, n_slots)).astype(BF16))
            data.append(lines[g * group + j])
        own = jnp.concatenate(own, axis=1)
        weights = jnp.concatenate([own, jnp.concatenate(both, axis=1)], axis=0)
        obs[...] += across(jnp.concatenate(data, axis=1), weights)
        pair[...] += across(weights, own)
        return carry

    lax.fori_loop(0, n_groups, add_group, 0)

    obs[:, :n_slots] = inner * obs[:, :n_slots] - side * obs[:, n_slots:]
    pair[:n_slots] = inner * pair[:n_slots] - side * pair[n_slots:]

    for line, at_end in ((0, band == 0), (n_lines - 1, band == n_band - 1)):
        @pl.when(at_end)
        def _(line=line):
            own = hot(padded[8 + line : 9 + line], n_slots).astype(BF16)
            excess = decay * decay * norm
            obs[:, :n_slots] -= excess * across(lines[line], own)
            pair[:n_slots] -= excess * across(own, own)

    for at, there in neighbours:
        @pl.when(there)
        def _(at=at):
            for copy in entries(at):
                copy.wait_send()
            pltpu.make_async_copy(dep_in.at[at], dep_in.at[at], entry_in.at[at]).wait()
            pltpu.make_async_copy(edge_in.at[at], edge_in.at[at], entry_in.at[2 + at]).wait()
            line = 0 if at == 0 else n_lines - 1
            theirs = edge_in[at][0:1]
            row = jnp.where(theirs >= 0, padded[8 + line : 9 + line], -1)
            mask = hot(row, n_slots).astype(BF16)
            obs[:, :n_slots] -= side * across(dep_in[at], mask)
            small[at] = across(mask, hot(theirs, n_slots).astype(BF16)).astype(BF16)

    def two(left, value):
        both = plain(left, jnp.concatenate(halves(value), axis=1))
        width = value.shape[1]
        return both[:, :width] + both[:, width:]

    measured = two(jac[...], two(prec[...], obs[:, :n_slots])).T
    high, low = halves(across(prec[...], jac[...]))
    metric_high, metric_low = halves(plain(jac[...], high) + plain(jac[...], low))
    pair_high, pair_low = halves(pair[:n_slots])

    settle(got, col_in)
    gotf[...] = got[...].astype(F32)
    mine[...] = jnp.concatenate([gotf[:, c, :] for c in range(cap)], axis=0).astype(BF16)
    for to, there in neighbours:
        @pl.when(there)
        def _(to=to):
            columns_to(to).start()
    block = mine[...]
    total[...] = plain(pair_high, block) + plain(pair_low, block)
    for at, there in neighbours:
        @pl.when(there)
        def _(at=at):
            columns_to(at).wait_send()
            pltpu.make_async_copy(mine_in.at[at], mine_in.at[at], row_in.at[at]).wait()
            total[...] -= side * plain(small[at], mine_in[at])
    mixed_high, mixed_low = halves(total[...])
    adjoint = (
        plain(mixed_high, metric_high) + (plain(mixed_low, metric_high) + plain(mixed_high, metric_low)) - measured
    )
    settle(sent, col_out)
    for c in range(cap):
        wide[:, c, :] = adjoint[c * n : (c + 1) * n]
    back[me] = wide[me]
    scatter(wide, back, adj_out, adj_in)
    settle(back, adj_in)
    settle(wide, adj_out)


def spread(back, rows, out):
    n, cap = rows.shape
    values = jnp.concatenate([back[:, c, :] for c in range(cap)], axis=0).T
    chosen = picks(rows, out.shape[1])
    high, low = halves(values)
    out[...] = plain(jnp.concatenate([high, low], axis=1), jnp.concatenate([chosen, chosen], axis=0))


def on_device(columns, departures, jacobian, chan_precision, send_rows, obs_slot, counts):
    n_band, n_lev = lax.axis_size("band"), lax.axis_size("lev")
    n = n_band * n_lev
    rows = send_rows[0]
    cap = rows.shape[1]
    n_slots = n * cap
    n_cols, prof = columns.shape
    dep = departures[0].transpose(0, 2, 1)
    n_lines, n_chan, n_pos = dep.shape
    group = 8
    in_vmem = pl.BlockSpec(memory_space=pltpu.VMEM)
    sem = pltpu.SemaphoreType.DMA
    back = pl.pallas_call(
        functools.partial(exchange, n_band, n_lev, group),
        out_shape=jax.ShapeDtypeStruct((n, cap, prof), F32),
        in_specs=[in_vmem, pl.BlockSpec(memory_space=pl.ANY)] + [in_vmem] * 5,
        out_specs=in_vmem,
        scratch_shapes=[
            pltpu.VMEM((n_lines, n_chan, n_pos), BF16),
            pltpu.VMEM((n_lines + 16, n_pos), jnp.int32),
            pltpu.VMEM((2, 8, n_pos), jnp.int32),
            pltpu.VMEM((2, 8, n_pos), jnp.int32),
            pltpu.VMEM((2, n_chan, n_pos), BF16),
            pltpu.VMEM((n, cap, prof), F32),
            pltpu.VMEM((n, cap, prof), BF16),
            pltpu.VMEM((n, cap, prof), BF16),
            pltpu.VMEM((n, cap, prof), F32),
            pltpu.VMEM((n_slots, prof), BF16),
            pltpu.VMEM((2, n_slots, prof), BF16),
            pltpu.VMEM((n_chan, 2 * n_slots), F32),
            pltpu.VMEM((2 * n_slots, n_slots), F32),
            pltpu.VMEM((2, n_slots, n_slots), BF16),
            pltpu.VMEM((n_slots, prof), F32),
            sem((n_lines // group,)),
            sem((4,)), sem((4,)), sem, sem, sem((2,)), sem((2,)), sem, sem,
        ],
        compiler_params=pltpu.CompilerParams(
            collective_id=0, has_side_effects=True, vmem_limit_bytes=60 * 1024 * 1024
        ),
    )(columns.T, dep, jacobian, chan_precision, rows, obs_slot[0], counts.reshape(n_lines, 1))
    result = pl.pallas_call(
        spread,
        out_shape=jax.ShapeDtypeStruct((prof, n_cols), F32),
        in_specs=[in_vmem, in_vmem],
        out_specs=in_vmem,
        compiler_params=pltpu.CompilerParams(vmem_limit_bytes=48 * 1024 * 1024),
    )(back, rows)
    return result.T


def solution(mesh):
    placed = (
        P(("band", "lev"), None),
        P("lev", "band", None, None),
        P(),
        P(),
        P(("band", "lev"), None, None),
        P("lev", "band", None),
        P("lev", "band"),
    )
    return jax.shard_map(
        on_device, mesh=mesh, in_specs=placed, out_specs=P(("band", "lev"), None), check_vma=False
    )
```

```python
import functools
import math

import jax
import jax.numpy as jnp
from jax import lax
from jax.experimental import pallas as pl
from jax.experimental.pallas import tpu as pltpu
from jax.sharding import PartitionSpec as P

MESH = pl.DeviceIdType.MESH
corr_length = 2.0
F32, BF16 = jnp.float32, jnp.bfloat16


def halves(value):
    high = value.astype(BF16)
    return high, (value - high.astype(F32)).astype(BF16)


def across(left, right):
    return lax.dot_general(left, right, (((1,), (1,)), ((), ())), preferred_element_type=F32)


def plain(left, right):
    return jnp.dot(left, right, preferred_element_type=F32)


def hot(row, count):
    return jnp.where(lax.broadcasted_iota(jnp.int32, (count, row.shape[1]), 0) == row, 1.0, 0.0)


def upright(row):
    shape = (row.shape[1], row.shape[1])
    same = lax.broadcasted_iota(jnp.int32, shape, 0) == lax.broadcasted_iota(jnp.int32, shape, 1)
    return jnp.sum(jnp.where(same, row.astype(F32), 0.0), axis=1, keepdims=True).astype(jnp.int32)


def picks(rows_ref, n_cols, first=0):
    cap, n = rows_ref.shape
    lanes = lax.broadcasted_iota(jnp.int32, (n, n_cols), 1) + first
    return jnp.concatenate(
        [jnp.where(lanes == upright(rows_ref[c : c + 1]), 1.0, 0.0) for c in range(cap)], axis=0
    ).astype(BF16)


def exchange(
    n_band, n_lev, group, cols_in, dep, jac_in, prec_in, rows, slots, counts, back,
    cols, jac, prec, lines, padded, edge, edge_in, dep_in, wide, sent, got, gotf, mine, mine_in,
    obs, pair, small, total, arg_sem, dep_sem, entry_out, entry_in, col_out, col_in, row_out, row_in, adj_out, adj_in,
):
    decay = math.exp(-1.0 / corr_length)
    norm = 1.0 / (1.0 - decay * decay)
    inner, side = (1.0 + decay * decay) * norm, decay * norm
    n = n_band * n_lev
    n_lines, n_chan, n_pos = dep.shape
    cap, prof = sent.shape[1], sent.shape[2]
    n_slots = n * cap
    band, lev = lax.axis_index("band"), lax.axis_index("lev")
    me = band * n_lev + lev
    has_prev, has_next = band > 0, band < n_band - 1

    fetched = [
        pltpu.make_async_copy(source, target, arg_sem.at[i])
        for i, (source, target) in enumerate(((cols_in, cols), (jac_in, jac), (prec_in, prec)))
    ]
    fetched[0].start()
    barrier = pltpu.get_barrier_semaphore()

    def greet(step, carry):
        other = lax.rem(me + step, n)
        pl.semaphore_signal(
            barrier, inc=1, device_id=(other // n_lev, lax.rem(other, n_lev)), device_id_type=MESH
        )
        return carry

    lax.fori_loop(1, n, greet, 0)

    n_groups = n_lines // group

    def load(g):
        part = pl.ds(g * group, group)
        return pltpu.make_async_copy(dep.at[part], lines.at[part], dep_sem.at[g])

    for g in range(n_groups):
        load(g).start()
    fetched[1].start()
    fetched[2].start()

    chosen = picks(rows, cols.shape[1])
    fetched[0].wait()
    gathered = across(chosen, cols[...])
    for c in range(cap):
        wide[:, c, :] = gathered[c * n : (c + 1) * n]
    sent[...] = wide[...].astype(BF16)
    got[me] = sent[me]

    numbers = slots[...]
    ordered = lax.rem(numbers, cap) * n + lax.div(numbers, cap)
    place = lax.broadcasted_iota(jnp.int32, (n_lines, n_pos), 1)
    ordered = jnp.where(place < upright(counts[...]), ordered, -1)
    nothing = jnp.full((8, n_pos), -1, jnp.int32)
    padded[0:8] = nothing
    padded[8 : 8 + n_lines] = ordered
    padded[8 + n_lines : 16 + n_lines] = nothing
    edge[0] = jnp.broadcast_to(ordered[0:1], (8, n_pos))
    edge[1] = jnp.broadcast_to(ordered[n_lines - 1 : n_lines], (8, n_pos))

    pl.semaphore_wait(barrier, n - 1)

    def scatter(blocks, target, out_sem, in_sem):
        def send(step, carry):
            other = lax.rem(me + step, n)
            pltpu.make_async_remote_copy(
                src_ref=blocks.at[other], dst_ref=target.at[me], send_sem=out_sem, recv_sem=in_sem,
                device_id=(other // n_lev, lax.rem(other, n_lev)), device_id_type=MESH,
            ).start()
            return carry

        lax.fori_loop(1, n, send, 0)

    def settle(blocks, sem):
        others = blocks.at[pl.ds(0, n - 1)]
        pltpu.make_async_copy(others, others, sem).wait()

    scatter(sent, got, col_out, col_in)

    def entries(to):
        line = 0 if to == 0 else n_lines - 1
        other = (band - 1 if to == 0 else band + 1, lev)
        place = 1 - to
        return (
            pltpu.make_async_remote_copy(
                src_ref=dep.at[line], dst_ref=dep_in.at[place], send_sem=entry_out.at[to],
                recv_sem=entry_in.at[place], device_id=other, device_id_type=MESH),
            pltpu.make_async_remote_copy(
                src_ref=edge.at[to], dst_ref=edge_in.at[place], send_sem=entry_out.at[2 + to],
                recv_sem=entry_in.at[2 + place], device_id=other, device_id_type=MESH),
        )

    def columns_to(to):
        other = (band - 1 if to == 0 else band + 1, lev)
        return pltpu.make_async_remote_copy(
            src_ref=mine, dst_ref=mine_in.at[1 - to], send_sem=row_out.at[to],
            recv_sem=row_in.at[1 - to], device_id=other, device_id_type=MESH)

    neighbours = ((0, has_prev), (1, has_next))
    for to, there in neighbours:
        @pl.when(there)
        def _(to=to):
            for copy in entries(to):
                copy.start()

    obs[...] = jnp.zeros_like(obs)
    pair[...] = jnp.zeros_like(pair)

    def add_group(g, carry):
        load(g).wait()
        near = padded[pl.ds(pl.multiple_of(g * group, 8), group + 16)]
        own, both, data = [], [], []
        for j in range(group):
            here = near[8 + j : 9 + j]
            before = jnp.where(here >= 0, near[7 + j : 8 + j], -1)
            after = jnp.where(here >= 0, near[9 + j : 10 + j], -1)
            own.append(hot(here, n_slots).astype(BF16))
            both.append((hot(before, n_slots) + hot(after, n_slots)).astype(BF16))
            data.append(lines[g * group + j])
        own = jnp.concatenate(own, axis=1)
        weights = jnp.concatenate([own, jnp.concatenate(both, axis=1)], axis=0)
        obs[...] += across(jnp.concatenate(data, axis=1), weights)
        pair[...] += across(weights, own)
        return carry

    early = n_groups - n_groups // 4
    lax.fori_loop(0, early, add_group, 0)
    settle(got, col_in)
    gotf[...] = got[...].astype(F32)
    mine[...] = jnp.concatenate([gotf[:, c, :] for c in range(cap)], axis=0).astype(BF16)
    for to, there in neighbours:
        @pl.when(there)
        def _(to=to):
            columns_to(to).start()
    lax.fori_loop(early, n_groups, add_group, 0)

    obs[:, :n_slots] = inner * obs[:, :n_slots] - side * obs[:, n_slots:]
    pair[:n_slots] = inner * pair[:n_slots] - side * pair[n_slots:]

    for line, at_end in ((0, band == 0), (n_lines - 1, band == n_band - 1)):
        @pl.when(at_end)
        def _(line=line):
            own = hot(padded[8 + line : 9 + line], n_slots).astype(BF16)
            excess = decay * decay * norm
            obs[:, :n_slots] -= excess * across(lines[line], own)
            pair[:n_slots] -= excess * across(own, own)

    for at, there in neighbours:
        @pl.when(there)
        def _(at=at):
            for copy in entries(at):
                copy.wait_send()
            pltpu.make_async_copy(dep_in.at[at], dep_in.at[at], entry_in.at[at]).wait()
            pltpu.make_async_copy(edge_in.at[at], edge_in.at[at], entry_in.at[2 + at]).wait()
            line = 0 if at == 0 else n_lines - 1
            theirs = edge_in[at][0:1]
            row = jnp.where(theirs >= 0, padded[8 + line : 9 + line], -1)
            mask = hot(row, n_slots).astype(BF16)
            obs[:, :n_slots] -= side * across(dep_in[at], mask)
            small[at] = across(mask, hot(theirs, n_slots).astype(BF16)).astype(BF16)

    fetched[1].wait()
    fetched[2].wait()

    def two(left, value):
        both = plain(left, jnp.concatenate(halves(value), axis=1))
        width = value.shape[1]
        return both[:, :width] + both[:, width:]

    measured = two(jac[...], two(prec[...], obs[:, :n_slots])).T
    high, low = halves(across(prec[...], jac[...]))
    metric_high, metric_low = halves(plain(jac[...], high) + plain(jac[...], low))
    pair_high, pair_low = halves(pair[:n_slots])

    block = mine[...]
    total[...] = plain(pair_high, block) + plain(pair_low, block)
    for at, there in neighbours:
        @pl.when(there)
        def _(at=at):
            columns_to(at).wait_send()
            pltpu.make_async_copy(mine_in.at[at], mine_in.at[at], row_in.at[at]).wait()
            total[...] -= side * plain(small[at], mine_in[at])
    mixed_high, mixed_low = halves(total[...])
    adjoint = (
        plain(mixed_high, metric_high) + (plain(mixed_low, metric_high) + plain(mixed_high, metric_low)) - measured
    )
    settle(sent, col_out)
    for c in range(cap):
        wide[:, c, :] = adjoint[c * n : (c + 1) * n]
    back[me] = wide[me]
    scatter(wide, back, adj_out, adj_in)
    settle(back, adj_in)
    settle(wide, adj_out)


def spread(back_in, rows, out, back, piece, in_sem, out_sem):
    fetch = pltpu.make_async_copy(back_in, back, in_sem)
    fetch.start()
    cap = rows.shape[0]
    parts, _, width = piece.shape
    chosen = [picks(rows, width, part * width) for part in range(parts)]
    fetch.wait()
    values = jnp.concatenate([back[:, c, :] for c in range(cap)], axis=0).T
    values = jnp.concatenate(halves(values), axis=1)
    copies = []
    for part in range(parts):
        piece[part] = plain(values, jnp.concatenate([chosen[part], chosen[part]], axis=0))
        copies.append(
            pltpu.make_async_copy(piece.at[part], out.at[:, part * width : (part + 1) * width], out_sem.at[part])
        )
        copies[part].start()
    for copy in copies:
        copy.wait()


def on_device(columns, departures, jacobian, chan_precision, send_rows, obs_slot, counts):
    n_band, n_lev = lax.axis_size("band"), lax.axis_size("lev")
    n = n_band * n_lev
    rows = send_rows[0].T
    cap = rows.shape[0]
    n_slots = n * cap
    n_cols, prof = columns.shape
    dep = departures[0].transpose(0, 2, 1)
    n_lines, n_chan, n_pos = dep.shape
    group, parts = 8, 4
    in_vmem = pl.BlockSpec(memory_space=pltpu.VMEM)
    anywhere = pl.BlockSpec(memory_space=pl.ANY)
    sem = pltpu.SemaphoreType.DMA
    back = pl.pallas_call(
        functools.partial(exchange, n_band, n_lev, group),
        out_shape=jax.ShapeDtypeStruct((n, cap, prof), F32),
        in_specs=[anywhere] * 4 + [in_vmem] * 3,
        out_specs=in_vmem,
        scratch_shapes=[
            pltpu.VMEM((prof, n_cols), BF16),
            pltpu.VMEM((prof, n_chan), BF16),
            pltpu.VMEM((n_chan, n_chan), BF16),
            pltpu.VMEM((n_lines, n_chan, n_pos), BF16),
            pltpu.VMEM((n_lines + 16, n_pos), jnp.int32),
            pltpu.VMEM((2, 8, n_pos), jnp.int32),
            pltpu.VMEM((2, 8, n_pos), jnp.int32),
            pltpu.VMEM((2, n_chan, n_pos), BF16),
            pltpu.VMEM((n, cap, prof), F32),
            pltpu.VMEM((n, cap, prof), BF16),
            pltpu.VMEM((n, cap, prof), BF16),
            pltpu.VMEM((n, cap, prof), F32),
            pltpu.VMEM((n_slots, prof), BF16),
            pltpu.VMEM((2, n_slots, prof), BF16),
            pltpu.VMEM((n_chan, 2 * n_slots), F32),
            pltpu.VMEM((2 * n_slots, n_slots), F32),
            pltpu.VMEM((2, n_slots, n_slots), BF16),
            pltpu.VMEM((n_slots, prof), F32),
            sem((3,)),
            sem((n_lines // group,)),
            sem((4,)), sem((4,)), sem, sem, sem((2,)), sem((2,)), sem, sem,
        ],
        compiler_params=pltpu.CompilerParams(
            collective_id=0, has_side_effects=True, vmem_limit_bytes=60 * 1024 * 1024
        ),
    )(columns.T, dep, jacobian, chan_precision, rows, obs_slot[0], counts)
    result = pl.pallas_call(
        spread,
        out_shape=jax.ShapeDtypeStruct((prof, n_cols), F32),
        in_specs=[anywhere, in_vmem],
        out_specs=anywhere,
        scratch_shapes=[
            pltpu.VMEM((n, cap, prof), F32),
            pltpu.VMEM((parts, prof, n_cols // parts), F32),
            sem,
            sem((parts,)),
        ],
        compiler_params=pltpu.CompilerParams(vmem_limit_bytes=60 * 1024 * 1024),
    )(back, rows)
    return result.T


def solution(mesh):
    placed = (
        P(("band", "lev"), None),
        P("lev", "band", None, None),
        P(),
        P(),
        P(("band", "lev"), None, None),
        P("lev", "band", None),
        P("lev", "band"),
    )
    return jax.shard_map(
        on_device, mesh=mesh, in_specs=placed, out_specs=P(("band", "lev"), None), check_vma=False
    )
```

```python
import functools
import math

import jax
import jax.numpy as jnp
from jax import lax
from jax.experimental import pallas as pl
from jax.experimental.pallas import tpu as pltpu
from jax.sharding import PartitionSpec as P

MESH = pl.DeviceIdType.MESH
corr_length = 2.0
F32, BF16 = jnp.float32, jnp.bfloat16


def halves(value):
    high = value.astype(BF16)
    return high, (value - high.astype(F32)).astype(BF16)


def across(left, right):
    return lax.dot_general(left, right, (((1,), (1,)), ((), ())), preferred_element_type=F32)


def plain(left, right):
    return jnp.dot(left, right, preferred_element_type=F32)


def hot(row, count):
    return jnp.where(lax.broadcasted_iota(jnp.int32, (count, row.shape[1]), 0) == row, 1.0, 0.0)


def upright(row):
    shape = (row.shape[1], row.shape[1])
    same = lax.broadcasted_iota(jnp.int32, shape, 0) == lax.broadcasted_iota(jnp.int32, shape, 1)
    return jnp.sum(jnp.where(same, row.astype(F32), 0.0), axis=1, keepdims=True).astype(jnp.int32)


def columns_of(rows_ref):
    return jnp.concatenate([upright(rows_ref[c : c + 1]) for c in range(rows_ref.shape[0])], axis=0)


def picks(wanted, n_cols, first=0):
    lanes = lax.broadcasted_iota(jnp.int32, (wanted.shape[0], n_cols), 1)
    return jnp.where(lanes == wanted - first, 1.0, 0.0).astype(BF16)


def exchange(
    n_band, n_lev, group, cols_in, dep, jac_in, prec_in, rows, slots, counts, back,
    cols, jac, prec, lines, padded, edge, edge_in, dep_in, wide, sent, got, gotf, mine, mine_in,
    obs, pair, small, total, arg_sem, dep_sem, entry_out, entry_in, col_out, col_in, row_out, row_in, adj_out, adj_in,
):
    decay = math.exp(-1.0 / corr_length)
    norm = 1.0 / (1.0 - decay * decay)
    inner, side = (1.0 + decay * decay) * norm, decay * norm
    n = n_band * n_lev
    n_lines, n_chan, n_pos = dep.shape
    cap, prof = sent.shape[1], sent.shape[2]
    n_slots = n * cap
    band, lev = lax.axis_index("band"), lax.axis_index("lev")
    me = band * n_lev + lev
    has_prev, has_next = band > 0, band < n_band - 1

    fetched = [
        pltpu.make_async_copy(source, target, arg_sem.at[i])
        for i, (source, target) in enumerate(((cols_in, cols), (jac_in, jac), (prec_in, prec)))
    ]
    fetched[0].start()
    barrier = pltpu.get_barrier_semaphore()

    def greet(step, carry):
        other = lax.rem(me + step, n)
        pl.semaphore_signal(
            barrier, inc=1, device_id=(other // n_lev, lax.rem(other, n_lev)), device_id_type=MESH
        )
        return carry

    lax.fori_loop(1, n, greet, 0)

    n_groups = n_lines // group

    def load(g):
        part = pl.ds(g * group, group)
        return pltpu.make_async_copy(dep.at[part], lines.at[part], dep_sem.at[g])

    for g in range(n_groups):
        load(g).start()
    fetched[1].start()
    fetched[2].start()

    chosen = picks(columns_of(rows), cols.shape[1])
    fetched[0].wait()
    gathered = across(chosen, cols[...])
    for c in range(cap):
        wide[:, c, :] = gathered[c * n : (c + 1) * n]
    sent[...] = wide[...].astype(BF16)
    got[me] = sent[me]

    numbers = slots[...]
    ordered = lax.rem(numbers, cap) * n + lax.div(numbers, cap)
    place = lax.broadcasted_iota(jnp.int32, (n_lines, n_pos), 1)
    ordered = jnp.where(place < upright(counts[...]), ordered, -1)
    nothing = jnp.full((8, n_pos), -1, jnp.int32)
    padded[0:8] = nothing
    padded[8 : 8 + n_lines] = ordered
    padded[8 + n_lines : 16 + n_lines] = nothing
    edge[0] = jnp.broadcast_to(ordered[0:1], (8, n_pos))
    edge[1] = jnp.broadcast_to(ordered[n_lines - 1 : n_lines], (8, n_pos))

    pl.semaphore_wait(barrier, n - 1)

    def scatter(blocks, target, out_sem, in_sem):
        def send(step, carry):
            other = lax.rem(me + step, n)
            pltpu.make_async_remote_copy(
                src_ref=blocks.at[other], dst_ref=target.at[me], send_sem=out_sem, recv_sem=in_sem,
                device_id=(other // n_lev, lax.rem(other, n_lev)), device_id_type=MESH,
            ).start()
            return carry

        lax.fori_loop(1, n, send, 0)

    def settle(blocks, sem):
        others = blocks.at[pl.ds(0, n - 1)]
        pltpu.make_async_copy(others, others, sem).wait()

    scatter(sent, got, col_out, col_in)

    def entries(to):
        line = 0 if to == 0 else n_lines - 1
        other = (band - 1 if to == 0 else band + 1, lev)
        place = 1 - to
        return (
            pltpu.make_async_remote_copy(
                src_ref=dep.at[line], dst_ref=dep_in.at[place], send_sem=entry_out.at[to],
                recv_sem=entry_in.at[place], device_id=other, device_id_type=MESH),
            pltpu.make_async_remote_copy(
                src_ref=edge.at[to], dst_ref=edge_in.at[place], send_sem=entry_out.at[2 + to],
                recv_sem=entry_in.at[2 + place], device_id=other, device_id_type=MESH),
        )

    def columns_to(to):
        other = (band - 1 if to == 0 else band + 1, lev)
        return pltpu.make_async_remote_copy(
            src_ref=mine, dst_ref=mine_in.at[1 - to], send_sem=row_out.at[to],
            recv_sem=row_in.at[1 - to], device_id=other, device_id_type=MESH)

    neighbours = ((0, has_prev), (1, has_next))
    for to, there in neighbours:
        @pl.when(there)
        def _(to=to):
            for copy in entries(to):
                copy.start()

    obs[...] = jnp.zeros_like(obs)
    pair[...] = jnp.zeros_like(pair)

    def add_group(g, carry):
        load(g).wait()
        near = padded[pl.ds(pl.multiple_of(g * group, 8), group + 16)]
        own, both, data = [], [], []
        for j in range(group):
            here = near[8 + j : 9 + j]
            before = jnp.where(here >= 0, near[7 + j : 8 + j], -1)
            after = jnp.where(here >= 0, near[9 + j : 10 + j], -1)
            own.append(hot(here, n_slots).astype(BF16))
            both.append((hot(before, n_slots) + hot(after, n_slots)).astype(BF16))
            data.append(lines[g * group + j])
        own = jnp.concatenate(own, axis=1)
        weights = jnp.concatenate([own, jnp.concatenate(both, axis=1)], axis=0)
        obs[...] += across(jnp.concatenate(data, axis=1), weights)
        pair[...] += across(weights, own)
        return carry

    early = n_groups - n_groups // 4
    lax.fori_loop(0, early, add_group, 0)
    settle(got, col_in)
    gotf[...] = got[...].astype(F32)
    arrived = jnp.concatenate([gotf[:, c, :] for c in range(cap)], axis=0)
    mine[...] = arrived.T.astype(BF16)
    for to, there in neighbours:
        @pl.when(there)
        def _(to=to):
            columns_to(to).start()
    lax.fori_loop(early, n_groups, add_group, 0)

    obs[:, :n_slots] = inner * obs[:, :n_slots] - side * obs[:, n_slots:]
    pair[:n_slots] = inner * pair[:n_slots] - side * pair[n_slots:]

    for line, at_end in ((0, band == 0), (n_lines - 1, band == n_band - 1)):
        @pl.when(at_end)
        def _(line=line):
            own = hot(padded[8 + line : 9 + line], n_slots).astype(BF16)
            excess = decay * decay * norm
            obs[:, :n_slots] -= excess * across(lines[line], own)
            pair[:n_slots] -= excess * across(own, own)

    for at, there in neighbours:
        @pl.when(there)
        def _(at=at):
            for copy in entries(at):
                copy.wait_send()
            pltpu.make_async_copy(dep_in.at[at], dep_in.at[at], entry_in.at[at]).wait()
            pltpu.make_async_copy(edge_in.at[at], edge_in.at[at], entry_in.at[2 + at]).wait()
            line = 0 if at == 0 else n_lines - 1
            theirs = edge_in[at][0:1]
            row = jnp.where(theirs >= 0, padded[8 + line : 9 + line], -1)
            mask = hot(row, n_slots).astype(BF16)
            obs[:, :n_slots] -= side * across(dep_in[at], mask)
            small[at] = across(mask, hot(theirs, n_slots).astype(BF16)).astype(BF16)

    fetched[1].wait()
    fetched[2].wait()

    def two(left, value):
        both = plain(left, jnp.concatenate(halves(value), axis=1))
        width = value.shape[1]
        return both[:, :width] + both[:, width:]

    measured = two(jac[...], two(prec[...], obs[:, :n_slots])).T
    high, low = halves(across(prec[...], jac[...]))
    metric_high, metric_low = halves(plain(jac[...], high) + plain(jac[...], low))
    pair_high, pair_low = halves(pair[:n_slots])

    block = mine[...]
    total[...] = across(pair_high, block) + across(pair_low, block)
    for at, there in neighbours:
        @pl.when(there)
        def _(at=at):
            columns_to(at).wait_send()
            pltpu.make_async_copy(mine_in.at[at], mine_in.at[at], row_in.at[at]).wait()
            total[...] -= side * across(small[at], mine_in[at])
    mixed_high, mixed_low = halves(total[...])
    adjoint = (
        plain(mixed_high, metric_high) + (plain(mixed_low, metric_high) + plain(mixed_high, metric_low)) - measured
    )
    settle(sent, col_out)
    for c in range(cap):
        wide[:, c, :] = adjoint[c * n : (c + 1) * n]
    back[me] = wide[me]
    scatter(wide, back, adj_out, adj_in)
    settle(back, adj_in)
    settle(wide, adj_out)


def spread(back_in, rows, out, back, piece, in_sem, out_sem):
    fetch = pltpu.make_async_copy(back_in, back, in_sem)
    fetch.start()
    cap = rows.shape[0]
    parts, _, width = piece.shape
    wanted = columns_of(rows)
    chosen = [picks(wanted, width, part * width) for part in range(parts)]
    fetch.wait()
    values = jnp.concatenate([back[:, c, :] for c in range(cap)], axis=0).T
    values = jnp.concatenate(halves(values), axis=1)
    copies = []
    for part in range(parts):
        piece[part] = plain(values, jnp.concatenate([chosen[part], chosen[part]], axis=0))
        copies.append(
            pltpu.make_async_copy(piece.at[part], out.at[:, part * width : (part + 1) * width], out_sem.at[part])
        )
        copies[part].start()
    for copy in copies:
        copy.wait()


def on_device(columns, departures, jacobian, chan_precision, send_rows, obs_slot, counts):
    n_band, n_lev = lax.axis_size("band"), lax.axis_size("lev")
    n = n_band * n_lev
    rows = send_rows[0].T
    cap = rows.shape[0]
    n_slots = n * cap
    n_cols, prof = columns.shape
    dep = departures[0].transpose(0, 2, 1)
    n_lines, n_chan, n_pos = dep.shape
    group, parts = 8, 2
    in_vmem = pl.BlockSpec(memory_space=pltpu.VMEM)
    anywhere = pl.BlockSpec(memory_space=pl.ANY)
    sem = pltpu.SemaphoreType.DMA
    back = pl.pallas_call(
        functools.partial(exchange, n_band, n_lev, group),
        out_shape=jax.ShapeDtypeStruct((n, cap, prof), F32),
        in_specs=[anywhere] * 4 + [in_vmem] * 3,
        out_specs=in_vmem,
        scratch_shapes=[
            pltpu.VMEM((prof, n_cols), BF16),
            pltpu.VMEM((prof, n_chan), BF16),
            pltpu.VMEM((n_chan, n_chan), BF16),
            pltpu.VMEM((n_lines, n_chan, n_pos), BF16),
            pltpu.VMEM((n_lines + 16, n_pos), jnp.int32),
            pltpu.VMEM((2, 8, n_pos), jnp.int32),
            pltpu.VMEM((2, 8, n_pos), jnp.int32),
            pltpu.VMEM((2, n_chan, n_pos), BF16),
            pltpu.VMEM((n, cap, prof), F32),
            pltpu.VMEM((n, cap, prof), BF16),
            pltpu.VMEM((n, cap, prof), BF16),
            pltpu.VMEM((n, cap, prof), F32),
            pltpu.VMEM((prof, n_slots), BF16),
            pltpu.VMEM((2, prof, n_slots), BF16),
            pltpu.VMEM((n_chan, 2 * n_slots), F32),
            pltpu.VMEM((2 * n_slots, n_slots), F32),
            pltpu.VMEM((2, n_slots, n_slots), BF16),
            pltpu.VMEM((n_slots, prof), F32),
            sem((3,)),
            sem((n_lines // group,)),
            sem((4,)), sem((4,)), sem, sem, sem((2,)), sem((2,)), sem, sem,
        ],
        compiler_params=pltpu.CompilerParams(
            collective_id=0, has_side_effects=True, vmem_limit_bytes=60 * 1024 * 1024
        ),
    )(columns.T, dep, jacobian, chan_precision, rows, obs_slot[0], counts)
    result = pl.pallas_call(
        spread,
        out_shape=jax.ShapeDtypeStruct((prof, n_cols), F32),
        in_specs=[anywhere, in_vmem],
        out_specs=anywhere,
        scratch_shapes=[
            pltpu.VMEM((n, cap, prof), F32),
            pltpu.VMEM((parts, prof, n_cols // parts), F32),
            sem,
            sem((parts,)),
        ],
        compiler_params=pltpu.CompilerParams(vmem_limit_bytes=60 * 1024 * 1024),
    )(back, rows)
    return result.T


def solution(mesh):
    placed = (
        P(("band", "lev"), None),
        P("lev", "band", None, None),
        P(),
        P(),
        P(("band", "lev"), None, None),
        P("lev", "band", None),
        P("lev", "band"),
    )
    return jax.shard_map(
        on_device, mesh=mesh, in_specs=placed, out_specs=P(("band", "lev"), None), check_vma=False
    )
```
